32 devices in a mesh: groups: 2 (over y), tensor: 4 (over z), dp: 4 (over x, core).
Axes of the slice: x: 2, y: 2, z: 4, core: 2. Of those that a mesh axis runs over, the one named last changes fastest.
Arguments:
- inputs: bfloat16 [1536, 6144], P(('groups', 'tensor')), parts along dimension 0, may hold values from -36 to 36
- ln_gain: float32 [6144], replicated, may hold values from 0.25 to 1.75
- w_query: bfloat16 [6144, 512], P('dp', 'tensor'), may hold values from -0.078125 to 0.078125
- w_keyval: bfloat16 [4, 1536, 1024], P('dp', 'tensor'), may hold values from -0.078125 to 0.078125
- w_gate: bfloat16 [6144, 1536], P('dp', 'tensor'), may hold values from -0.078125 to 0.078125
- w_up: bfloat16 [6144, 1536], P('dp', 'tensor'), may hold values from -0.078125 to 0.078125
- w_out: bfloat16 [512, 6144], P('tensor', 'dp'), may hold values from -0.25 to 0.25
- w_down: bfloat16 [1536, 6144], P('tensor', 'dp'), may hold values from -0.15625 to 0.15625
- cache_keys: bfloat16 [8, 4, 256, 128], P(('groups', 'dp')), parts along dimension 0, may hold values from -500 to 500
- cache_values: bfloat16 [8, 4, 256, 128], P(('groups', 'dp')), parts along dimension 0, may hold values from -5 to 5
- lengths: int32 [8], P(('groups', 'dp')), parts along dimension 0, may hold values from 64 to 256, as said below
- starts: int32 [8], P(('groups', 'dp')), parts along dimension 0, may hold values from 64 to 511, as said below
Outputs:
- layer_out: bfloat16 [1536, 6144], P(('groups', 'tensor'), 'dp'), parts along dimension 0
The draws below stay inside these ranges and needn't reach their ends.
There are 2 independent parts, one for each index of `groups`. The reference program is written for one: setup_inputs(seed, part) draws one part's arguments, and reference() takes and returns one part's arrays. A program takes and returns all parts, laid end to end along the dimension named above; an argument that names none is the same for every part. Nothing has to cross between parts.
Inputs may be any that keep to these rules, and one draw needn't show every extreme that they name: `lengths`: at most 256 live slots, and one sequence has exactly 256 in every draw. `starts`: a sequence's first new position is at least its number of live cache slots and less than that number plus 256; cached keys belong to earlier positions.
All inputs are finite; a program needn't handle non-finite values.
Results may differ from the reference program's by a relative error of at most 0.0054.
Values may be sent and summed in bfloat16 or wider, within the bound.
A program may use at most 64 MiB of HBM per device.

```python
import math
import jax
import jax.numpy as jnp
from jax import lax

D = 6144
HEAD = 128
KV_HEADS = 4
SPAN = 192
CACHE = 256
HEADS = 4
FF = 1536
KV_COLS = 1024
SEQS = 4
TOKENS = 768
N_DP = 4


def lengths_and_gaps(key):
    len_key, pick_key, gap_key = jax.random.split(key, 3)
    drawn_len = jax.random.randint(len_key, (SEQS,), CACHE // 4, CACHE + 1)
    chosen = jax.random.randint(pick_key, (), 0, SEQS)
    is_chosen = jnp.arange(SEQS) == chosen
    drawn_len = jnp.where(is_chosen, CACHE, drawn_len)
    position_gap = jax.random.randint(gap_key, (SEQS,), 0, CACHE)
    position_gap = jnp.where(is_chosen, CACHE - 1, position_gap)
    return (drawn_len.astype(jnp.int32), position_gap.astype(jnp.int32))


def draw_lengths(key, part):
    kept_len, position_gap = lengths_and_gaps(key)
    return kept_len


def draw_starts(key, part):
    kept_len, position_gap = lengths_and_gaps(key)
    return kept_len + position_gap


def draw_inputs(key, part):
    key = jax.random.fold_in(key, 11)
    row_key, col_key, base_key = jax.random.split(key, 3)
    row_scale = jnp.exp(jax.random.uniform(row_key, (TOKENS, 1), jnp.float32, math.log(0.3), math.log(3.0)))
    col_scale = jnp.exp(jax.random.uniform(col_key, (1, D), jnp.float32, math.log(0.3), math.log(3.0)))
    base_vals = jnp.clip(jax.random.normal(base_key, (TOKENS, D), jnp.float32), -4.0, 4.0)
    return (base_vals * row_scale * col_scale).astype(jnp.bfloat16)


def draw_cache_keys(key, part):
    key = jax.random.fold_in(key, 23)
    base_key = jax.random.fold_in(key, 0)
    key_shape = (SEQS, KV_HEADS, CACHE, HEAD)
    base_vals = jnp.clip(jax.random.normal(base_key, key_shape, jnp.float32), -4.0, 4.0)
    return base_vals.astype(jnp.bfloat16)


def level_of(key, extent, cuts, least, largest):
    loudness = 1.0
    for position, shards_of in cuts:
        draws = jax.random.uniform(jax.random.fold_in(jax.random.fold_in(key, 6), position), (shards_of,), jnp.float32, least / len(cuts), largest / len(cuts))
        loudness = loudness * jnp.repeat(jnp.exp(draws), extent[position] // shards_of).reshape((-1,) + (1,) * (len(extent) - 1 - position))
    return loudness


def scatter_about(key, extent, deviation, limit, cuts=(), held_as=jnp.bfloat16):
    array = deviation * jax.random.normal(key, extent, jnp.float32)
    if cuts:
        array = array * level_of(key, extent, cuts, -0.22, 0.18)
    return jnp.clip(array, -limit, limit).astype(held_as)


def setup_inputs(seed: int = 0, part: int = 0) -> dict:
    streams_of = jax.random.split(jax.random.key(seed), 13)
    part_splits = jax.random.split(jax.random.fold_in(streams_of[12], part), 13)
    return {
        "inputs": draw_inputs(jax.random.fold_in(jax.random.fold_in(streams_of[12], part), 71), part),
        "ln_gain": jnp.clip(1.0 + 0.15 * jax.random.normal(streams_of[1], (D,), jnp.float32), 0.25, 1.75),
        "w_query": scatter_about(streams_of[2], (D, HEADS * HEAD), D ** -0.5, 0.078125, ((0, 4), (1, 4))),
        "w_keyval": scatter_about(streams_of[3], (N_DP, D // N_DP, KV_COLS), D ** -0.5, 0.078125, ((0, 4), (1, 4))),
        "w_gate": scatter_about(streams_of[4], (D, FF), D ** -0.5, 0.078125, ((0, 4), (1, 4))),
        "w_up": scatter_about(streams_of[5], (D, FF), D ** -0.5, 0.078125, ((0, 4), (1, 4))),
        "w_out": scatter_about(streams_of[6], (HEADS * HEAD, D), (HEADS * HEAD) ** -0.5, 0.25, ((0, 4), (1, 4))),
        "w_down": scatter_about(streams_of[7], (FF, D), FF ** -0.5, 0.15625, ((0, 4), (1, 4))),
        "cache_keys": draw_cache_keys(jax.random.fold_in(jax.random.fold_in(streams_of[12], part), 71), part),
        "cache_values": scatter_about(part_splits[9], (SEQS, KV_HEADS, CACHE, HEAD), 1.0, 5.0, ((0, 4),)),
        "lengths": draw_lengths(jax.random.fold_in(jax.random.fold_in(streams_of[12], part), 71), part),
        "starts": draw_starts(jax.random.fold_in(jax.random.fold_in(streams_of[12], part), 71), part),
    }


rope_base = 75000000.0
norm_eps = 1e-05

def layer_norm(row_values, gain_values):
    widened = row_values.astype(jnp.float32)
    centered = widened - lax.optimization_barrier(jnp.mean(widened, axis=-1, keepdims=True))
    spread_sq = lax.optimization_barrier(jnp.mean(centered * centered, axis=-1, keepdims=True))
    return (centered * lax.rsqrt(spread_sq + norm_eps) * gain_values.astype(jnp.float32)).astype(jnp.bfloat16)

def rotate(values, positions):
    head_width = values.shape[-1]
    half_width = head_width // 2
    frequency = rope_base ** (-2.0 * jnp.arange(half_width, dtype=jnp.float32) / head_width)
    angles = positions[..., None] * frequency
    paired = values.reshape(values.shape[:-1] + (half_width, 2))
    even_part = paired[..., 0]
    odd_part = paired[..., 1]
    cosine = jnp.cos(angles)
    sine_vals = jnp.sin(angles)
    turned = jnp.stack([even_part * cosine - odd_part * sine_vals, even_part * sine_vals + odd_part * cosine], axis=-1)
    return turned.reshape(values.shape)

def reference(inputs, ln_gain, w_query, w_keyval, w_gate, w_up, w_out, w_down, cache_keys, cache_values, lengths, starts):
    normed = layer_norm(inputs, ln_gain)
    query = jnp.dot(normed, w_query, preferred_element_type=jnp.float32)
    keyval = jnp.dot(normed, w_keyval.reshape(D, KV_COLS), preferred_element_type=jnp.float32)
    gate_proj = jnp.dot(normed, w_gate, preferred_element_type=jnp.float32)
    up_proj = jnp.dot(normed, w_up, preferred_element_type=jnp.float32)
    hidden_act = (jax.nn.silu(gate_proj) * up_proj).astype(jnp.bfloat16)
    offsets = jnp.arange(SPAN, dtype=jnp.int32)
    positions = (starts[:, None] + offsets[None, :]).astype(jnp.float32)
    query_heads = query.reshape(SEQS, SPAN, HEADS, HEAD)
    rotated_query = rotate(query_heads, positions[:, :, None]).astype(jnp.bfloat16)
    key_heads = keyval[:, :KV_HEADS * HEAD].reshape(SEQS, SPAN, KV_HEADS, HEAD)
    new_keys = rotate(key_heads, positions[:, :, None]).astype(jnp.bfloat16)
    new_values = keyval[:, KV_HEADS * HEAD:].reshape(SEQS, SPAN, KV_HEADS, HEAD).astype(jnp.bfloat16)
    group_size = HEADS // KV_HEADS
    keys_full = jnp.repeat(new_keys, group_size, axis=2).astype(jnp.float32)
    values_full = jnp.repeat(new_values, group_size, axis=2).astype(jnp.float32)
    cached_k = jnp.repeat(cache_keys, group_size, axis=1).astype(jnp.float32)
    cached_v = jnp.repeat(cache_values, group_size, axis=1).astype(jnp.float32)
    scale_factor = HEAD ** (-0.5)
    query_wide = rotated_query.astype(jnp.float32)
    cached_scores = jnp.einsum('sqhd,shkd->shqk', query_wide, cached_k) * scale_factor
    new_scores = jnp.einsum('sqhd,skhd->shqk', query_wide, keys_full) * scale_factor
    slot_index = jnp.arange(CACHE, dtype=jnp.int32)
    live_slot = slot_index[None, :] < lengths[:, None]
    causal = offsets[:, None] >= offsets[None, :]
    cached_scores = jnp.where(live_slot[:, None, None, :], cached_scores, -jnp.inf)
    new_scores = jnp.where(causal[None, None], new_scores, -jnp.inf)
    row_peak = jnp.maximum(lax.optimization_barrier(jnp.max(cached_scores, axis=-1, keepdims=True)), lax.optimization_barrier(jnp.max(new_scores, axis=-1, keepdims=True)))
    cached_exp = jnp.exp(cached_scores - row_peak)
    new_exp = jnp.exp(new_scores - row_peak)
    denominator = lax.optimization_barrier(jnp.sum(cached_exp, axis=-1, keepdims=True)) + lax.optimization_barrier(jnp.sum(new_exp, axis=-1, keepdims=True))
    cached_prob = (cached_exp / denominator).astype(jnp.bfloat16).astype(jnp.float32)
    new_prob = (new_exp / denominator).astype(jnp.bfloat16).astype(jnp.float32)
    attended = jnp.einsum('shqk,shkd->sqhd', cached_prob, cached_v) + jnp.einsum('shqk,skhd->sqhd', new_prob, values_full)
    attended = attended.astype(jnp.bfloat16).reshape(TOKENS, HEADS * HEAD)
    branches = jnp.dot(attended, w_out, preferred_element_type=jnp.float32) + jnp.dot(hidden_act, w_down, preferred_element_type=jnp.float32)
    return (inputs.astype(jnp.float32) + branches).astype(jnp.bfloat16)
```

```python
import functools

import jax
import jax.numpy as jnp
from jax import lax
from jax.experimental import pallas as pl
from jax.experimental.pallas import tpu as pltpu
from jax.sharding import PartitionSpec as P

SPAN = 192


rope_base = 75000000.0
norm_eps = 1e-05


def layer_norm(row_values, gain_values):
    widened = row_values.astype(jnp.float32)
    centered = widened - jnp.mean(widened, axis=-1, keepdims=True)
    spread_sq = jnp.mean(centered * centered, axis=-1, keepdims=True)
    return (centered * lax.rsqrt(spread_sq + norm_eps) * gain_values).astype(jnp.bfloat16)


def rotate(values, positions):
    head_width = values.shape[-1]
    half_width = head_width // 2
    frequency = rope_base ** (-2.0 * jnp.arange(half_width, dtype=jnp.float32) / head_width)
    angles = positions[..., None] * frequency
    paired = values.reshape(values.shape[:-1] + (half_width, 2))
    even_part = paired[..., 0]
    odd_part = paired[..., 1]
    cosine = jnp.cos(angles)
    sine_vals = jnp.sin(angles)
    turned = jnp.stack(
        [even_part * cosine - odd_part * sine_vals, even_part * sine_vals + odd_part * cosine],
        axis=-1,
    )
    return turned.reshape(values.shape)


def on_device(
    inputs,
    ln_gain,
    w_query,
    w_keyval,
    w_gate,
    w_up,
    w_out,
    w_down,
    cache_keys,
    cache_values,
    lengths,
    starts,
):
    tensor_index = lax.axis_index("tensor")
    data_index = lax.axis_index("dp")
    tensor_count = lax.axis_size("tensor")
    block_width = w_gate.shape[0]
    sub_width = w_keyval.shape[1]
    head_width = w_query.shape[1]
    ffn_width = w_gate.shape[1]
    kv_heads = cache_keys.shape[1]
    kv_group = tensor_index // (tensor_count // kv_heads)
    normed = layer_norm(inputs, ln_gain)
    own_block = lax.dynamic_slice_in_dim(normed, data_index * block_width, block_width, 1)
    every_row = lax.all_gather(own_block, "tensor", axis=0, tiled=True)
    offsets = jnp.arange(SPAN, dtype=jnp.int32)
    positions = (starts[0] + offsets).astype(jnp.float32)
    kv_rows = lax.dynamic_slice_in_dim(every_row, tensor_index * sub_width, sub_width, 1)
    kv_term = jnp.dot(kv_rows, w_keyval[0], preferred_element_type=jnp.float32)
    keyval = lax.psum(kv_term, ("tensor", "dp"))
    own_keyval = lax.dynamic_slice_in_dim(keyval, data_index * SPAN, SPAN, 0)
    key_cols = lax.dynamic_slice_in_dim(own_keyval, kv_group * head_width, head_width, 1)
    value_cols = lax.dynamic_slice_in_dim(
        own_keyval, (kv_heads + kv_group) * head_width, head_width, 1
    )
    pieces = [
        jnp.dot(every_row, w_query, preferred_element_type=jnp.float32),
        jnp.dot(every_row, w_gate, preferred_element_type=jnp.float32),
        jnp.dot(every_row, w_up, preferred_element_type=jnp.float32),
    ]
    projected = lax.psum_scatter(
        jnp.concatenate(pieces, axis=1), "dp", scatter_dimension=0, tiled=True
    )
    query = projected[:, :head_width]
    gate_proj = projected[:, head_width : head_width + ffn_width]
    up_proj = projected[:, head_width + ffn_width : head_width + 2 * ffn_width]
    hidden_act = (jax.nn.silu(gate_proj) * up_proj).astype(jnp.bfloat16)
    rotated_query = rotate(query, positions).astype(jnp.bfloat16)
    new_keys = rotate(key_cols, positions).astype(jnp.bfloat16)
    new_values = value_cols.astype(jnp.bfloat16)
    cached_k = lax.dynamic_index_in_dim(cache_keys[0], kv_group, 0, keepdims=False)
    cached_v = lax.dynamic_index_in_dim(cache_values[0], kv_group, 0, keepdims=False)
    scale_factor = head_width ** (-0.5)
    cached_scores = (
        jnp.einsum("qd,kd->qk", rotated_query, cached_k, preferred_element_type=jnp.float32)
        * scale_factor
    )
    new_scores = (
        jnp.einsum("qd,kd->qk", rotated_query, new_keys, preferred_element_type=jnp.float32)
        * scale_factor
    )
    slot_index = jnp.arange(cached_k.shape[0], dtype=jnp.int32)
    cached_scores = jnp.where(slot_index[None, :] < lengths[0], cached_scores, -jnp.inf)
    causal = offsets[:, None] >= offsets[None, :]
    new_scores = jnp.where(causal, new_scores, -jnp.inf)
    row_peak = jnp.maximum(
        jnp.max(cached_scores, axis=-1, keepdims=True), jnp.max(new_scores, axis=-1, keepdims=True)
    )
    cached_exp = jnp.exp(cached_scores - row_peak)
    new_exp = jnp.exp(new_scores - row_peak)
    denominator = jnp.sum(cached_exp, axis=-1, keepdims=True) + jnp.sum(
        new_exp, axis=-1, keepdims=True
    )
    cached_prob = (cached_exp / denominator).astype(jnp.bfloat16)
    new_prob = (new_exp / denominator).astype(jnp.bfloat16)
    attended = (
        jnp.dot(cached_prob, cached_v, preferred_element_type=jnp.float32)
        + jnp.dot(new_prob, new_values, preferred_element_type=jnp.float32)
    ).astype(jnp.bfloat16)
    joined = jnp.concatenate([attended, hidden_act], axis=1)
    gathered_piece = lax.all_gather(joined, "dp", axis=0, tiled=True)
    partial_terms = jnp.dot(
        gathered_piece[:, :head_width], w_out, preferred_element_type=jnp.float32
    ) + jnp.dot(gathered_piece[:, head_width:], w_down, preferred_element_type=jnp.float32)
    row_share = inputs.shape[0]
    residual = lax.dynamic_slice_in_dim(inputs, data_index * block_width, block_width, 1).astype(
        jnp.float32
    )
    summed = lax.psum(partial_terms, "tensor")
    own_sum = lax.dynamic_slice_in_dim(summed, tensor_index * row_share, row_share, 0)
    return (residual + own_sum).astype(jnp.bfloat16)

GATHER_CHUNKS = 2
REDUCE_CHUNKS = 4


def fused_kernel(
    sizes,
    x_hbm,
    gain_ref,
    wq_hbm,
    wkv_hbm,
    wg_hbm,
    wu_hbm,
    wo_hbm,
    wd_hbm,
    ck_hbm,
    cv_hbm,
    cos_ref,
    sin_ref,
    bias_ref,
    out_ref,
    x_buf,
    rows_buf,
    w_in,
    wo_buf,
    wd_buf,
    ck_buf,
    cv_buf,
    part_send,
    part_own,
    part_recv,
    att_buf,
    hid_buf,
    acc,
    from_left,
    from_right,
    sum_send,
    x_sem,
    load_sem,
    kv_send,
    kv_recv,
    row_send_l,
    row_send_r,
    row_recv,
    part_ssem,
    part_rsem,
    joined_ssem,
    joined_rsem,
    sum_ssem,
    left_rsem,
    right_rsem,
):
    n, span, head, ffn, block, sub = sizes
    t = lax.axis_index("tensor")
    d = lax.axis_index("dp")
    mesh_id = pl.DeviceIdType.MESH
    last = n - 1
    ga = span // GATHER_CHUNKS
    ra = span // REDUCE_CHUNKS
    own_cols = pl.ds(pl.multiple_of(d * block, 128), block)

    def rows_of(chunk, size):
        return pl.ds(pl.multiple_of(chunk * size, size), size)

    def remote(src, dst, ssem, rsem, axis, index):
        return pltpu.make_async_remote_copy(
            src_ref=src,
            dst_ref=dst,
            send_sem=ssem,
            recv_sem=rsem,
            device_id={axis: index},
            device_id_type=mesh_id,
        )

    def x_copy(chunk):
        rows = rows_of(chunk, ga)
        return pltpu.make_async_copy(x_hbm.at[rows], x_buf.at[rows], x_sem.at[chunk])

    own_sub = pl.ds(pl.multiple_of(t * sub, sub), sub)
    key_cols = pl.ds(pl.multiple_of(t * head, head), head)
    value_cols = pl.ds(pl.multiple_of((n + t) * head, head), head)
    gate_at = 3 * head
    up_at = 3 * head + ffn
    loads = [
        (wq_hbm, w_in.at[:, pl.ds(0, head)]),
        (wg_hbm, w_in.at[:, pl.ds(gate_at, ffn)]),
        (wu_hbm, w_in.at[:, pl.ds(up_at, ffn)]),
        (wkv_hbm.at[:, key_cols], w_in.at[own_sub, pl.ds(head, head)]),
        (wkv_hbm.at[:, value_cols], w_in.at[own_sub, pl.ds(2 * head, head)]),
        (wo_hbm, wo_buf),
        (wd_hbm, wd_buf),
        (ck_hbm.at[t], ck_buf),
        (cv_hbm.at[t], cv_buf),
    ]
    load_copies = [
        pltpu.make_async_copy(a, b, load_sem.at[i]) for i, (a, b) in enumerate(loads)
    ]

    def kv_copy(peer, kind, slot):
        cols = pl.ds(pl.multiple_of((kind * n + peer) * head, head), head)
        return remote(
            wkv_hbm.at[:, cols],
            w_in.at[own_sub, pl.ds((1 + kind) * head, head)],
            kv_send.at[slot, kind],
            kv_recv.at[t, kind],
            "tensor",
            peer,
        )

    def kv_arrival(peer, kind):
        rows = pl.ds(pl.multiple_of(peer * sub, sub), sub)
        dst = w_in.at[rows, pl.ds((1 + kind) * head, head)]
        return remote(dst, dst, kv_send.at[0, kind], kv_recv.at[peer, kind], "tensor", peer)

    def row_copy(s, chunk, to_left):
        view = rows_buf.at[s, rows_of(chunk, ga)]
        sems = row_send_l if to_left else row_send_r
        target = t - 1 if to_left else t + 1
        return remote(view, view, sems.at[s, chunk], row_recv.at[s, chunk], "tensor", target)

    def part_copy(s, chunk):
        rows = rows_of(chunk, ga)
        return remote(
            part_send.at[s, rows],
            part_recv.at[d, rows],
            part_ssem.at[s, chunk],
            part_rsem.at[d, chunk],
            "dp",
            s,
        )

    def part_arrival(peer, chunk):
        dst = part_recv.at[peer, rows_of(chunk, ga)]
        return remote(
            dst, dst, part_ssem.at[peer, chunk], part_rsem.at[peer, chunk], "dp", peer
        )

    def joined_copy(s, peer, slot, kind):
        view = (att_buf if kind else hid_buf).at[s]
        return remote(
            view, view, joined_ssem.at[slot, kind], joined_rsem.at[s, kind], "dp", peer
        )

    def sum_copy(s, chunk, to_left):
        rows = rows_of(chunk, ra)
        dst = (from_right if to_left else from_left).at[s, rows]
        sems = right_rsem if to_left else left_rsem
        target = t - 1 if to_left else t + 1
        return remote(
            sum_send.at[s, rows], dst, sum_ssem.at[s, chunk], sems.at[s, chunk], "tensor", target
        )

    for chunk in range(GATHER_CHUNKS):
        x_copy(chunk).start()
    for copy in load_copies:
        copy.start()

    barrier = pltpu.get_barrier_semaphore()
    for p in range(1, n):
        pl.semaphore_signal(
            barrier, inc=1, device_id={"tensor": lax.rem(t + p, n)}, device_id_type=mesh_id
        )
        pl.semaphore_signal(
            barrier, inc=1, device_id={"dp": lax.rem(d + p, n)}, device_id_type=mesh_id
        )
    pl.semaphore_wait(barrier, 2 * (n - 1))

    for p in range(1, n):
        for kind in range(2):
            kv_copy(lax.rem(t + p, n), kind, p).start()

    norm_rows = 16
    gain = gain_ref[:, own_cols]

    @pl.loop(0, GATHER_CHUNKS)
    def _(chunk):
        x_copy(chunk).wait()

        @pl.loop(0, ga // norm_rows)
        def _(i):
            rows = pl.ds(pl.multiple_of(chunk * ga + i * norm_rows, norm_rows), norm_rows)
            wide = x_buf[rows, :].astype(jnp.float32)
            mean = jnp.mean(wide, axis=-1, keepdims=True)
            centered = wide - mean
            spread = jnp.mean(centered * centered, axis=-1, keepdims=True)
            own = x_buf[rows, own_cols].astype(jnp.float32) - mean
            normed = (own * lax.rsqrt(spread + norm_eps) * gain).astype(jnp.bfloat16)
            rows_buf[t, rows, :] = normed

        @pl.when(t > 0)
        def _():
            row_copy(t, chunk, True).start()

        @pl.when(t < last)
        def _():
            row_copy(t, chunk, False).start()

    for copy in load_copies:
        copy.wait()
    for p in range(1, n):
        for kind in range(2):
            kv_arrival(lax.rem(t + p, n), kind).wait_recv()

    inner = jnp.where((t > 0) & (t < last), 1, 0)
    near = jnp.where(t < 2, 1, 0)

    def mirrored(v):
        return near * v + (1 - near) * (last - v)

    def rotated(v):
        lane = lax.broadcasted_iota(jnp.int32, v.shape, 1)
        swapped = jnp.where(
            lax.rem(lane, 2) == 0, pltpu.roll(v, head - 1, 1), pltpu.roll(v, 1, 1)
        )
        return v * cos_ref[...] + swapped * sin_ref[...]

    def attend(s):
        for p in range(1, n):
            peer = lax.rem(d + p, n)
            for chunk in range(GATHER_CHUNKS):
                part_arrival(peer, chunk).wait_recv()

        def total(first, width):
            cols = pl.ds(first, width)
            result = part_own[:, cols]
            for p in range(1, n):
                result = result + part_recv[lax.rem(d + p, n), :, cols].astype(jnp.float32)
            return result

        gate = total(gate_at, ffn)
        up = total(up_at, ffn)
        hid_buf[s] = (gate / (1.0 + jnp.exp(-gate)) * up).astype(jnp.bfloat16)
        for p in range(1, n):
            joined_copy(s, lax.rem(d + p, n), p, 0).start()
        query = rotated(total(0, head)).astype(jnp.bfloat16)
        new_keys = rotated(total(head, head)).astype(jnp.bfloat16)
        new_values = total(2 * head, head).astype(jnp.bfloat16)
        scale = head ** (-0.5)
        contract = (((1,), (1,)), ((), ()))
        cached = (
            lax.dot_general(query, ck_buf[...], contract, preferred_element_type=jnp.float32)
            * scale
            + bias_ref[...]
        )
        fresh = (
            lax.dot_general(query, new_keys, contract, preferred_element_type=jnp.float32) * scale
        )
        row_at = lax.broadcasted_iota(jnp.int32, (span, span), 0)
        col_at = lax.broadcasted_iota(jnp.int32, (span, span), 1)
        fresh = jnp.where(row_at >= col_at, fresh, -jnp.inf)
        peak = jnp.maximum(
            jnp.max(cached, axis=-1, keepdims=True), jnp.max(fresh, axis=-1, keepdims=True)
        )
        cached_exp = jnp.exp(cached - peak)
        fresh_exp = jnp.exp(fresh - peak)
        denominator = jnp.sum(cached_exp, axis=-1, keepdims=True) + jnp.sum(
            fresh_exp, axis=-1, keepdims=True
        )
        cached_prob = (cached_exp / denominator).astype(jnp.bfloat16)
        fresh_prob = (fresh_exp / denominator).astype(jnp.bfloat16)
        att_buf[s] = (
            jnp.dot(cached_prob, cv_buf[...], preferred_element_type=jnp.float32)
            + jnp.dot(fresh_prob, new_values, preferred_element_type=jnp.float32)
        ).astype(jnp.bfloat16)
        for p in range(1, n):
            joined_copy(s, lax.rem(d + p, n), p, 1).start()

    def project(s):
        @pl.loop(0, GATHER_CHUNKS)
        def _(chunk):
            @pl.when(s != t)
            def _():
                row_copy(s, chunk, True).wait_recv()

            @pl.when((s < t) & (t < last))
            def _():
                row_copy(s, chunk, False).start()

            @pl.when((s > t) & (t > 0))
            def _():
                row_copy(s, chunk, True).start()

            rows = rows_of(chunk, ga)
            term = jnp.dot(rows_buf[s, rows, :], w_in[...], preferred_element_type=jnp.float32)

            @pl.when(s == d)
            def _():
                part_own[rows, :] = term

            @pl.when(s != d)
            def _():
                part_send[s, rows, :] = term.astype(jnp.bfloat16)
                part_copy(s, chunk).start()

        @pl.when(s == d)
        def _():
            attend(s)

    col_tile = 512

    def combine(s):
        @pl.when(s != d)
        def _():
            joined_copy(s, s, 1, 0).wait_recv()
            joined_copy(s, s, 1, 1).wait_recv()

        @pl.loop(0, block // col_tile)
        def _(i):
            cols = pl.ds(pl.multiple_of(i * col_tile, col_tile), col_tile)
            acc[:, cols] = jnp.dot(
                att_buf[s], wo_buf[:, cols], preferred_element_type=jnp.float32
            ) + jnp.dot(hid_buf[s], wd_buf[:, cols], preferred_element_type=jnp.float32)

        @pl.loop(0, REDUCE_CHUNKS)
        def _(chunk):
            rows = rows_of(chunk, ra)

            @pl.when((t > 0) & (t <= s))
            def _():
                sum_copy(s, chunk, False).wait_recv()
                acc[rows, :] += from_left[s, rows, :].astype(jnp.float32)

            @pl.when((t < last) & (t >= s))
            def _():
                sum_copy(s, chunk, True).wait_recv()
                acc[rows, :] += from_right[s, rows, :].astype(jnp.float32)

            @pl.when(t == s)
            def _():
                residual = x_buf[rows, own_cols].astype(jnp.float32)
                out_ref[rows, :] = (residual + acc[rows, :]).astype(jnp.bfloat16)

            @pl.when(t != s)
            def _():
                sum_send[s, rows, :] = acc[rows, :].astype(jnp.bfloat16)

            @pl.when(t < s)
            def _():
                sum_copy(s, chunk, False).start()

            @pl.when(t > s)
            def _():
                sum_copy(s, chunk, True).start()

    @pl.loop(0, 2 * n)
    def _(slot):
        outer_p = (slot < 3) | (slot == 5)
        inner_p = slot < 4
        is_p = jnp.where(inner == 1, jnp.where(inner_p, 1, 0), jnp.where(outer_p, 1, 0))
        event_p = jnp.where(slot < 4, slot, 3)
        event_c = jnp.where(inner == 1, slot - 4, jnp.where(slot < 5, slot - 3, slot - 4))

        @pl.when(is_p == 1)
        def _():
            swapped = jnp.where((inner == 1) & (event_p < 2), 1 - event_p, event_p)
            project(mirrored(swapped))

        @pl.when(is_p == 0)
        def _():
            ends = lax.rem(event_c + 1, n)
            middle = jnp.where(event_c < 2, 2 - event_c, jnp.where(event_c == 2, 3, 0))
            combine(mirrored(jnp.where(inner == 1, middle, ends)))

    for p in range(1, n):
        peer_t = lax.rem(t + p, n)
        peer_d = lax.rem(d + p, n)
        for kind in range(2):
            kv_copy(peer_t, kind, p).wait_send()
            joined_copy(d, peer_d, p, kind).wait_send()
        for chunk in range(GATHER_CHUNKS):
            part_copy(peer_d, chunk).wait_send()

    @pl.loop(0, n)
    def _(s):
        for chunk in range(GATHER_CHUNKS):
            @pl.when((s >= t) & (t > 0))
            def _():
                row_copy(s, chunk, True).wait_send()

            @pl.when((s <= t) & (t < last))
            def _():
                row_copy(s, chunk, False).wait_send()

        for chunk in range(REDUCE_CHUNKS):
            @pl.when(t < s)
            def _():
                sum_copy(s, chunk, False).wait_send()

            @pl.when(t > s)
            def _():
                sum_copy(s, chunk, True).wait_send()


def fused_on_device(
    inputs,
    ln_gain,
    w_query,
    w_keyval,
    w_gate,
    w_up,
    w_out,
    w_down,
    cache_keys,
    cache_values,
    lengths,
    starts,
):
    n = lax.axis_size("tensor")
    block, head = w_query.shape
    ffn = w_gate.shape[1]
    sub = w_keyval.shape[1]
    cache = cache_keys.shape[2]
    width = 3 * head + 2 * ffn
    lane = jnp.arange(head, dtype=jnp.int32)
    pair = (lane // 2).astype(jnp.float32)
    frequency = rope_base ** (-2.0 * pair / head)
    positions = (starts[0] + jnp.arange(SPAN, dtype=jnp.int32)).astype(jnp.float32)
    angles = positions[:, None] * frequency
    cosine = jnp.cos(angles)
    sine = jnp.sin(angles) * jnp.where(lane % 2 == 0, -1.0, 1.0)
    bias = jnp.where(jnp.arange(cache) < lengths[0], 0.0, -jnp.inf).astype(jnp.float32)
    bf16, f32 = jnp.bfloat16, jnp.float32
    anywhere = pl.BlockSpec(memory_space=pl.ANY)
    vmem = pl.BlockSpec(memory_space=pltpu.VMEM)
    dma = pltpu.SemaphoreType.DMA
    return pl.pallas_call(
        functools.partial(fused_kernel, (n, SPAN, head, ffn, block, sub)),
        out_shape=jax.ShapeDtypeStruct((SPAN, block), bf16),
        in_specs=[anywhere, vmem] + [anywhere] * 8 + [vmem] * 3,
        out_specs=vmem,
        scratch_shapes=[
            pltpu.VMEM(inputs.shape, bf16),
            pltpu.VMEM((n, SPAN, block), bf16),
            pltpu.VMEM((block, width), bf16),
            pltpu.VMEM(w_out.shape, bf16),
            pltpu.VMEM(w_down.shape, bf16),
            pltpu.VMEM((cache, head), bf16),
            pltpu.VMEM((cache, head), bf16),
            pltpu.VMEM((n, SPAN, width), bf16),
            pltpu.VMEM((SPAN, width), f32),
            pltpu.VMEM((n, SPAN, width), bf16),
            pltpu.VMEM((n, SPAN, head), bf16),
            pltpu.VMEM((n, SPAN, ffn), bf16),
            pltpu.VMEM((SPAN, block), f32),
            pltpu.VMEM((n, SPAN, block), bf16),
            pltpu.VMEM((n, SPAN, block), bf16),
            pltpu.VMEM((n, SPAN, block), bf16),
            dma((GATHER_CHUNKS,)),
            dma((9,)),
            dma((n, 2)),
            dma((n, 2)),
            dma((n, GATHER_CHUNKS)),
            dma((n, GATHER_CHUNKS)),
            dma((n, GATHER_CHUNKS)),
            dma((n, GATHER_CHUNKS)),
            dma((n, GATHER_CHUNKS)),
            dma((n, 2)),
            dma((n, 2)),
            dma((n, REDUCE_CHUNKS)),
            dma((n, REDUCE_CHUNKS)),
            dma((n, REDUCE_CHUNKS)),
        ],
        compiler_params=pltpu.CompilerParams(
            collective_id=0, has_side_effects=True, vmem_limit_bytes=48 * 1024 * 1024
        ),
    )(
        inputs,
        ln_gain[None, :],
        w_query,
        w_keyval[0],
        w_gate,
        w_up,
        w_out,
        w_down,
        cache_keys[0],
        cache_values[0],
        cosine,
        sine,
        bias[None, :],
    )


def solution(mesh):
    fits = mesh.shape["tensor"] == mesh.shape["dp"] == 4
    return jax.shard_map(
        fused_on_device if fits else on_device,
        mesh=mesh,
        in_specs=(
            P(("groups", "tensor"), None),
            P(),
            P("dp", "tensor"),
            P("dp", "tensor", None),
            P("dp", "tensor"),
            P("dp", "tensor"),
            P("tensor", "dp"),
            P("tensor", "dp"),
            P(("groups", "dp"), None, None, None),
            P(("groups", "dp"), None, None, None),
            P(("groups", "dp")),
            P(("groups", "dp")),
        ),
        out_specs=P(("groups", "tensor"), "dp"),
        check_vma=False,
    )
```

```python
import functools

import jax
import jax.numpy as jnp
from jax import lax
from jax.experimental import pallas as pl
from jax.experimental.pallas import tpu as pltpu
from jax.sharding import PartitionSpec as P

SPAN = 192


rope_base = 75000000.0
norm_eps = 1e-05


def layer_norm(row_values, gain_values):
    widened = row_values.astype(jnp.float32)
    centered = widened - jnp.mean(widened, axis=-1, keepdims=True)
    spread_sq = jnp.mean(centered * centered, axis=-1, keepdims=True)
    return (centered * lax.rsqrt(spread_sq + norm_eps) * gain_values).astype(jnp.bfloat16)


def rotate(values, positions):
    head_width = values.shape[-1]
    half_width = head_width // 2
    frequency = rope_base ** (-2.0 * jnp.arange(half_width, dtype=jnp.float32) / head_width)
    angles = positions[..., None] * frequency
    paired = values.reshape(values.shape[:-1] + (half_width, 2))
    even_part = paired[..., 0]
    odd_part = paired[..., 1]
    cosine = jnp.cos(angles)
    sine_vals = jnp.sin(angles)
    turned = jnp.stack(
        [even_part * cosine - odd_part * sine_vals, even_part * sine_vals + odd_part * cosine],
        axis=-1,
    )
    return turned.reshape(values.shape)


def on_device(
    inputs,
    ln_gain,
    w_query,
    w_keyval,
    w_gate,
    w_up,
    w_out,
    w_down,
    cache_keys,
    cache_values,
    lengths,
    starts,
):
    tensor_index = lax.axis_index("tensor")
    data_index = lax.axis_index("dp")
    tensor_count = lax.axis_size("tensor")
    block_width = w_gate.shape[0]
    sub_width = w_keyval.shape[1]
    head_width = w_query.shape[1]
    ffn_width = w_gate.shape[1]
    kv_heads = cache_keys.shape[1]
    kv_group = tensor_index // (tensor_count // kv_heads)
    normed = layer_norm(inputs, ln_gain)
    own_block = lax.dynamic_slice_in_dim(normed, data_index * block_width, block_width, 1)
    every_row = lax.all_gather(own_block, "tensor", axis=0, tiled=True)
    offsets = jnp.arange(SPAN, dtype=jnp.int32)
    positions = (starts[0] + offsets).astype(jnp.float32)
    kv_rows = lax.dynamic_slice_in_dim(every_row, tensor_index * sub_width, sub_width, 1)
    kv_term = jnp.dot(kv_rows, w_keyval[0], preferred_element_type=jnp.float32)
    keyval = lax.psum(kv_term, ("tensor", "dp"))
    own_keyval = lax.dynamic_slice_in_dim(keyval, data_index * SPAN, SPAN, 0)
    key_cols = lax.dynamic_slice_in_dim(own_keyval, kv_group * head_width, head_width, 1)
    value_cols = lax.dynamic_slice_in_dim(
        own_keyval, (kv_heads + kv_group) * head_width, head_width, 1
    )
    pieces = [
        jnp.dot(every_row, w_query, preferred_element_type=jnp.float32),
        jnp.dot(every_row, w_gate, preferred_element_type=jnp.float32),
        jnp.dot(every_row, w_up, preferred_element_type=jnp.float32),
    ]
    projected = lax.psum_scatter(
        jnp.concatenate(pieces, axis=1), "dp", scatter_dimension=0, tiled=True
    )
    query = projected[:, :head_width]
    gate_proj = projected[:, head_width : head_width + ffn_width]
    up_proj = projected[:, head_width + ffn_width : head_width + 2 * ffn_width]
    hidden_act = (jax.nn.silu(gate_proj) * up_proj).astype(jnp.bfloat16)
    rotated_query = rotate(query, positions).astype(jnp.bfloat16)
    new_keys = rotate(key_cols, positions).astype(jnp.bfloat16)
    new_values = value_cols.astype(jnp.bfloat16)
    cached_k = lax.dynamic_index_in_dim(cache_keys[0], kv_group, 0, keepdims=False)
    cached_v = lax.dynamic_index_in_dim(cache_values[0], kv_group, 0, keepdims=False)
    scale_factor = head_width ** (-0.5)
    cached_scores = (
        jnp.einsum("qd,kd->qk", rotated_query, cached_k, preferred_element_type=jnp.float32)
        * scale_factor
    )
    new_scores = (
        jnp.einsum("qd,kd->qk", rotated_query, new_keys, preferred_element_type=jnp.float32)
        * scale_factor
    )
    slot_index = jnp.arange(cached_k.shape[0], dtype=jnp.int32)
    cached_scores = jnp.where(slot_index[None, :] < lengths[0], cached_scores, -jnp.inf)
    causal = offsets[:, None] >= offsets[None, :]
    new_scores = jnp.where(causal, new_scores, -jnp.inf)
    row_peak = jnp.maximum(
        jnp.max(cached_scores, axis=-1, keepdims=True), jnp.max(new_scores, axis=-1, keepdims=True)
    )
    cached_exp = jnp.exp(cached_scores - row_peak)
    new_exp = jnp.exp(new_scores - row_peak)
    denominator = jnp.sum(cached_exp, axis=-1, keepdims=True) + jnp.sum(
        new_exp, axis=-1, keepdims=True
    )
    cached_prob = (cached_exp / denominator).astype(jnp.bfloat16)
    new_prob = (new_exp / denominator).astype(jnp.bfloat16)
    attended = (
        jnp.dot(cached_prob, cached_v, preferred_element_type=jnp.float32)
        + jnp.dot(new_prob, new_values, preferred_element_type=jnp.float32)
    ).astype(jnp.bfloat16)
    joined = jnp.concatenate([attended, hidden_act], axis=1)
    gathered_piece = lax.all_gather(joined, "dp", axis=0, tiled=True)
    partial_terms = jnp.dot(
        gathered_piece[:, :head_width], w_out, preferred_element_type=jnp.float32
    ) + jnp.dot(gathered_piece[:, head_width:], w_down, preferred_element_type=jnp.float32)
    row_share = inputs.shape[0]
    residual = lax.dynamic_slice_in_dim(inputs, data_index * block_width, block_width, 1).astype(
        jnp.float32
    )
    summed = lax.psum(partial_terms, "tensor")
    own_sum = lax.dynamic_slice_in_dim(summed, tensor_index * row_share, row_share, 0)
    return (residual + own_sum).astype(jnp.bfloat16)

GATHER_CHUNKS = 2
REDUCE_CHUNKS = 6
LEAD = 3


def fused_kernel(
    sizes,
    x_hbm,
    gain_ref,
    wq_hbm,
    wkv_hbm,
    wg_hbm,
    wu_hbm,
    wo_hbm,
    wd_hbm,
    ck_hbm,
    cv_hbm,
    cos_ref,
    sin_ref,
    bias_ref,
    out_ref,
    x_buf,
    rows_buf,
    w_in,
    wo_buf,
    wd_buf,
    ck_buf,
    cv_buf,
    part_send,
    part_own,
    part_recv,
    att_buf,
    hid_buf,
    acc,
    from_left,
    from_right,
    sum_send,
    x_sem,
    load_sem,
    kv_send,
    kv_recv,
    share_send,
    share_recv,
    row_send_l,
    row_send_r,
    row_recv,
    part_ssem,
    part_rsem,
    joined_ssem,
    joined_rsem,
    sum_ssem,
    left_rsem,
    right_rsem,
):
    n, span, head, ffn, block, sub = sizes
    t = lax.axis_index("tensor")
    d = lax.axis_index("dp")
    g = lax.axis_index("groups")
    mesh_id = pl.DeviceIdType.MESH
    last = n - 1
    ga = span // GATHER_CHUNKS
    ra = span // REDUCE_CHUNKS
    own_cols = pl.ds(pl.multiple_of(d * block, 128), block)

    def rows_of(chunk, size):
        return pl.ds(pl.multiple_of(chunk * size, size), size)

    def remote(src, dst, ssem, rsem, axis, index):
        return pltpu.make_async_remote_copy(
            src_ref=src,
            dst_ref=dst,
            send_sem=ssem,
            recv_sem=rsem,
            device_id={axis: index},
            device_id_type=mesh_id,
        )

    def x_copy(chunk):
        rows = rows_of(chunk, ga)
        return pltpu.make_async_copy(x_hbm.at[rows], x_buf.at[rows], x_sem.at[chunk])

    own_sub = pl.ds(pl.multiple_of(t * sub, sub), sub)
    key_cols = pl.ds(pl.multiple_of(t * head, head), head)
    value_cols = pl.ds(pl.multiple_of((n + t) * head, head), head)
    gate_at = 3 * head
    up_at = 3 * head + ffn
    loads = [
        (wq_hbm, w_in.at[:, pl.ds(0, head)]),
        (wg_hbm, w_in.at[:, pl.ds(gate_at, ffn)]),
        (wu_hbm, w_in.at[:, pl.ds(up_at, ffn)]),
        (wkv_hbm.at[:, key_cols], w_in.at[own_sub, pl.ds(head, head)]),
        (wkv_hbm.at[:, value_cols], w_in.at[own_sub, pl.ds(2 * head, head)]),
        (wo_hbm, wo_buf),
        (wd_hbm, wd_buf),
        (ck_hbm.at[t], ck_buf),
        (cv_hbm.at[t], cv_buf),
    ]
    load_copies = [
        pltpu.make_async_copy(a, b, load_sem.at[i]) for i, (a, b) in enumerate(loads)
    ]

    half = sub // 2

    def kv_part(owner, kind, group):
        rows = pl.ds(pl.multiple_of(owner * sub + group * half, half), half)
        return w_in.at[rows, pl.ds((1 + kind) * head, head)]

    def kv_copy(peer, kind, slot):
        cols = pl.ds(pl.multiple_of((kind * n + peer) * head, head), head)
        rows = pl.ds(pl.multiple_of(g * half, half), half)
        return remote(
            wkv_hbm.at[rows, cols],
            kv_part(t, kind, g),
            kv_send.at[slot, kind],
            kv_recv.at[t, kind],
            "tensor",
            peer,
        )

    def kv_arrival(peer, kind):
        dst = kv_part(peer, kind, g)
        return remote(dst, dst, kv_send.at[0, kind], kv_recv.at[peer, kind], "tensor", peer)

    def kv_share(peer, kind, slot):
        view = kv_part(peer, kind, g)
        return remote(
            view, view, share_send.at[slot, kind], share_recv.at[peer, kind], "groups", 1 - g
        )

    def kv_shared(peer, kind):
        dst = kv_part(peer, kind, 1 - g)
        return remote(
            dst, dst, share_send.at[0, kind], share_recv.at[peer, kind], "groups", 1 - g
        )

    def row_copy(s, chunk, to_left):
        view = rows_buf.at[s, rows_of(chunk, ga)]
        sems = row_send_l if to_left else row_send_r
        target = t - 1 if to_left else t + 1
        return remote(view, view, sems.at[s, chunk], row_recv.at[s, chunk], "tensor", target)

    def part_copy(s, chunk):
        rows = rows_of(chunk, ga)
        return remote(
            part_send.at[s, rows],
            part_recv.at[d, rows],
            part_ssem.at[s, chunk],
            part_rsem.at[d, chunk],
            "dp",
            s,
        )

    def part_arrival(peer, chunk):
        dst = part_recv.at[peer, rows_of(chunk, ga)]
        return remote(
            dst, dst, part_ssem.at[peer, chunk], part_rsem.at[peer, chunk], "dp", peer
        )

    def joined_copy(s, peer, slot, kind):
        view = (att_buf if kind else hid_buf).at[s]
        return remote(
            view, view, joined_ssem.at[slot, kind], joined_rsem.at[s, kind], "dp", peer
        )

    def sum_copy(s, chunk, to_left):
        rows = rows_of(chunk, ra)
        dst = (from_right if to_left else from_left).at[s, rows]
        sems = right_rsem if to_left else left_rsem
        target = t - 1 if to_left else t + 1
        return remote(
            sum_send.at[s, rows], dst, sum_ssem.at[s, chunk], sems.at[s, chunk], "tensor", target
        )

    for chunk in range(GATHER_CHUNKS):
        x_copy(chunk).start()
    for copy in load_copies:
        copy.start()

    barrier = pltpu.get_barrier_semaphore()
    for p in range(1, n):
        pl.semaphore_signal(
            barrier, inc=1, device_id={"tensor": lax.rem(t + p, n)}, device_id_type=mesh_id
        )
        pl.semaphore_signal(
            barrier, inc=1, device_id={"dp": lax.rem(d + p, n)}, device_id_type=mesh_id
        )
    pl.semaphore_signal(barrier, inc=1, device_id={"groups": 1 - g}, device_id_type=mesh_id)
    pl.semaphore_wait(barrier, 2 * (n - 1) + 1)

    for p in range(1, n):
        for kind in range(2):
            kv_copy(lax.rem(t + p, n), kind, p).start()

    norm_rows = 16
    gain = gain_ref[:, own_cols]

    @pl.loop(0, GATHER_CHUNKS)
    def _(chunk):
        x_copy(chunk).wait()

        @pl.loop(0, ga // norm_rows)
        def _(i):
            rows = pl.ds(pl.multiple_of(chunk * ga + i * norm_rows, norm_rows), norm_rows)
            wide = x_buf[rows, :].astype(jnp.float32)
            mean = jnp.mean(wide, axis=-1, keepdims=True)
            centered = wide - mean
            spread = jnp.mean(centered * centered, axis=-1, keepdims=True)
            own = x_buf[rows, own_cols].astype(jnp.float32) - mean
            normed = (own * lax.rsqrt(spread + norm_eps) * gain).astype(jnp.bfloat16)
            rows_buf[t, rows, :] = normed

        @pl.when(t > 0)
        def _():
            row_copy(t, chunk, True).start()

        @pl.when(t < last)
        def _():
            row_copy(t, chunk, False).start()

    for copy in load_copies:
        copy.wait()

    def share_weights():
        for p in range(1, n):
            for kind in range(2):
                kv_arrival(lax.rem(t + p, n), kind).wait_recv()
                kv_share(lax.rem(t + p, n), kind, p).start()

    def wait_weights():
        for p in range(1, n):
            for kind in range(2):
                kv_shared(lax.rem(t + p, n), kind).wait_recv()

    inner = jnp.where((t > 0) & (t < last), 1, 0)
    near = jnp.where(t < 2, 1, 0)

    def mirrored(v):
        return near * v + (1 - near) * (last - v)

    def rotated(v):
        lane = lax.broadcasted_iota(jnp.int32, v.shape, 1)
        swapped = jnp.where(
            lax.rem(lane, 2) == 0, pltpu.roll(v, head - 1, 1), pltpu.roll(v, 1, 1)
        )
        return v * cos_ref[...] + swapped * sin_ref[...]

    def attend(s):
        for p in range(1, n):
            peer = lax.rem(d + p, n)
            for chunk in range(GATHER_CHUNKS):
                part_arrival(peer, chunk).wait_recv()

        def total(first, width):
            cols = pl.ds(first, width)
            result = part_own[:, cols]
            for p in range(1, n):
                result = result + part_recv[lax.rem(d + p, n), :, cols].astype(jnp.float32)
            return result

        gate = total(gate_at, ffn)
        up = total(up_at, ffn)
        hid_buf[s] = (gate / (1.0 + jnp.exp(-gate)) * up).astype(jnp.bfloat16)
        for p in range(1, n):
            joined_copy(s, lax.rem(d + p, n), p, 0).start()
        query = rotated(total(0, head)).astype(jnp.bfloat16)
        new_keys = rotated(total(head, head)).astype(jnp.bfloat16)
        new_values = total(2 * head, head).astype(jnp.bfloat16)
        scale = head ** (-0.5)
        contract = (((1,), (1,)), ((), ()))
        cached = (
            lax.dot_general(query, ck_buf[...], contract, preferred_element_type=jnp.float32)
            * scale
            + bias_ref[...]
        )
        fresh = (
            lax.dot_general(query, new_keys, contract, preferred_element_type=jnp.float32) * scale
        )
        row_at = lax.broadcasted_iota(jnp.int32, (span, span), 0)
        col_at = lax.broadcasted_iota(jnp.int32, (span, span), 1)
        fresh = jnp.where(row_at >= col_at, fresh, -jnp.inf)
        peak = jnp.maximum(
            jnp.max(cached, axis=-1, keepdims=True), jnp.max(fresh, axis=-1, keepdims=True)
        )
        cached_exp = jnp.exp(cached - peak)
        fresh_exp = jnp.exp(fresh - peak)
        denominator = jnp.sum(cached_exp, axis=-1, keepdims=True) + jnp.sum(
            fresh_exp, axis=-1, keepdims=True
        )
        cached_prob = (cached_exp / denominator).astype(jnp.bfloat16)
        fresh_prob = (fresh_exp / denominator).astype(jnp.bfloat16)
        att_buf[s] = (
            jnp.dot(cached_prob, cv_buf[...], preferred_element_type=jnp.float32)
            + jnp.dot(fresh_prob, new_values, preferred_element_type=jnp.float32)
        ).astype(jnp.bfloat16)
        for p in range(1, n):
            joined_copy(s, lax.rem(d + p, n), p, 1).start()

    def forward(s):
        @pl.loop(0, GATHER_CHUNKS)
        def _(chunk):
            row_copy(s, chunk, True).wait_recv()

            @pl.when((s < t) & (t < last))
            def _():
                row_copy(s, chunk, False).start()

            @pl.when((s > t) & (t > 0))
            def _():
                row_copy(s, chunk, True).start()

    def project(s):
        @pl.loop(0, GATHER_CHUNKS)
        def _(chunk):
            rows = rows_of(chunk, ga)
            term = jnp.dot(rows_buf[s, rows, :], w_in[...], preferred_element_type=jnp.float32)

            @pl.when(s == d)
            def _():
                part_own[rows, :] = term

            @pl.when(s != d)
            def _():
                part_send[s, rows, :] = term.astype(jnp.bfloat16)
                part_copy(s, chunk).start()

    col_tile = 512

    def combine(s):
        @pl.when(s != d)
        def _():
            joined_copy(s, s, 1, 0).wait_recv()

        @pl.loop(0, block // col_tile)
        def _(i):
            cols = pl.ds(pl.multiple_of(i * col_tile, col_tile), col_tile)
            acc[s, :, cols] = jnp.dot(
                hid_buf[s], wd_buf[:, cols], preferred_element_type=jnp.float32
            )

        @pl.when(s != d)
        def _():
            joined_copy(s, s, 1, 1).wait_recv()

        @pl.loop(0, block // col_tile)
        def _(i):
            cols = pl.ds(pl.multiple_of(i * col_tile, col_tile), col_tile)
            acc[s, :, cols] += jnp.dot(
                att_buf[s], wo_buf[:, cols], preferred_element_type=jnp.float32
            )

    def pass_on(s, chunk):
        rows = rows_of(chunk, ra)
        place = (jnp.where(t < s, s - t, t - s) - 1) * REDUCE_CHUNKS + chunk

        @pl.when((inner == 0) & (t != s) & (place >= 2))
        def _():
            far = (place - 2) // REDUCE_CHUNKS + 1
            before = lax.rem(place - 2, REDUCE_CHUNKS)

            @pl.when(t < s)
            def _():
                sum_copy(t + far, before, False).wait_send()

            @pl.when(t > s)
            def _():
                sum_copy(t - far, before, True).wait_send()

        @pl.when((t > 0) & (t <= s))
        def _():
            sum_copy(s, chunk, False).wait_recv()
            acc[s, rows, :] += from_left[s, rows, :].astype(jnp.float32)

        @pl.when((t < last) & (t >= s))
        def _():
            sum_copy(s, chunk, True).wait_recv()
            acc[s, rows, :] += from_right[s, rows, :].astype(jnp.float32)

        @pl.when(t == s)
        def _():
            residual = x_buf[rows, own_cols].astype(jnp.float32)
            out_ref[rows, :] = (residual + acc[s, rows, :]).astype(jnp.bfloat16)

        @pl.when(t != s)
        def _():
            sum_send[s, rows, :] = acc[s, rows, :].astype(jnp.bfloat16)

        @pl.when(t < s)
        def _():
            sum_copy(s, chunk, False).start()

        @pl.when(t > s)
        def _():
            sum_copy(s, chunk, True).start()

    plans = (
        "V0W0P0A0F1P1A1F2P2C0S0A2F3P3C1L1A3H1C2S2C3S3",
        "V0F1F2W0P0A0P1P2F3A1A2P3A3C0C2C1S0C3D2D3S1N0",
    )
    plans = [[plan[i : i + 2] for i in range(0, len(plan), 2)] for plan in plans]
    kinds = "PACSDLHFVWN"

    def looked_up(slot, values):
        found = 0
        for i, pair in enumerate(zip(*values)):
            picked = pair[0] if pair[0] == pair[1] else jnp.where(inner == 1, pair[1], pair[0])
            found = jnp.where(slot == i, picked, found)
        return found

    p_order = ((0, 1, 2, 3), (1, 0, 2, 3))
    c_order = ((1, 2, 3, 0), (2, 1, 3, 0))
    step_kinds = [[kinds.index(step[0]) for step in plan] for plan in plans]
    step_rows = [
        [
            (p_order if step[0] in "PAF" else c_order)[which][int(step[1])]
            for step in plan
        ]
        for which, plan in enumerate(plans)
    ]

    @pl.loop(0, len(plans[0]))
    def _(slot):
        kind = looked_up(slot, step_kinds)
        s = mirrored(looked_up(slot, step_rows))

        @pl.when(kind == 0)
        def _():
            project(s)

        @pl.when((kind == 1) & (s == d))
        def _():
            attend(s)

        @pl.when(kind == 2)
        def _():
            combine(s)

        @pl.when(kind == 7)
        def _():
            forward(s)

        @pl.when(kind == 8)
        def _():
            share_weights()

        @pl.when(kind == 9)
        def _():
            wait_weights()

        @pl.when((kind >= 3) & (kind <= 6))
        def _():
            first = mirrored(c_order[1][2])
            second = mirrored(c_order[1][3])
            late = jnp.where(s == second, 1, 0)
            half_way = REDUCE_CHUNKS // 2
            lead = min(LEAD, REDUCE_CHUNKS)
            start = jnp.where(kind == 6, half_way, 0)
            stop = jnp.where(kind == 5, half_way, REDUCE_CHUNKS)

            @pl.loop(start, stop)
            def _(i):
                at = late * REDUCE_CHUNKS + i
                mixed = at - lead
                in_turns = (mixed >= 0) & (mixed < 2 * (REDUCE_CHUNKS - lead))
                take_first = (mixed < 0) | (in_turns & (lax.rem(at + lead, 2) == 1))
                later = jnp.where(take_first, lead + mixed // 2, mixed // 2)
                chunk = jnp.where(
                    in_turns, later, jnp.where(mixed < 0, at, at - REDUCE_CHUNKS)
                )
                turn = jnp.where(take_first, first, second)
                pass_on(jnp.where(kind == 4, turn, s), jnp.where(kind == 4, chunk, i))

    for p in range(1, n):
        peer_t = lax.rem(t + p, n)
        peer_d = lax.rem(d + p, n)
        for kind in range(2):
            kv_copy(peer_t, kind, p).wait_send()
            kv_share(peer_t, kind, p).wait_send()
            joined_copy(d, peer_d, p, kind).wait_send()
        for chunk in range(GATHER_CHUNKS):
            part_copy(peer_d, chunk).wait_send()

    @pl.loop(0, n)
    def _(s):
        for chunk in range(GATHER_CHUNKS):
            @pl.when((s >= t) & (t > 0))
            def _():
                row_copy(s, chunk, True).wait_send()

            @pl.when((s <= t) & (t < last))
            def _():
                row_copy(s, chunk, False).wait_send()

        for chunk in range(REDUCE_CHUNKS):
            tail = chunk >= REDUCE_CHUNKS - 2

            @pl.when((t < s) & ((inner == 1) | ((s - t == last) & tail)))
            def _():
                sum_copy(s, chunk, False).wait_send()

            @pl.when((t > s) & ((inner == 1) | ((t - s == last) & tail)))
            def _():
                sum_copy(s, chunk, True).wait_send()


def fused_on_device(
    inputs,
    ln_gain,
    w_query,
    w_keyval,
    w_gate,
    w_up,
    w_out,
    w_down,
    cache_keys,
    cache_values,
    lengths,
    starts,
):
    n = lax.axis_size("tensor")
    block, head = w_query.shape
    ffn = w_gate.shape[1]
    sub = w_keyval.shape[1]
    cache = cache_keys.shape[2]
    width = 3 * head + 2 * ffn
    lane = jnp.arange(head, dtype=jnp.int32)
    pair = (lane // 2).astype(jnp.float32)
    frequency = rope_base ** (-2.0 * pair / head)
    positions = (starts[0] + jnp.arange(SPAN, dtype=jnp.int32)).astype(jnp.float32)
    angles = positions[:, None] * frequency
    cosine = jnp.cos(angles)
    sine = jnp.sin(angles) * jnp.where(lane % 2 == 0, -1.0, 1.0)
    bias = jnp.where(jnp.arange(cache) < lengths[0], 0.0, -jnp.inf).astype(jnp.float32)
    bf16, f32 = jnp.bfloat16, jnp.float32
    anywhere = pl.BlockSpec(memory_space=pl.ANY)
    vmem = pl.BlockSpec(memory_space=pltpu.VMEM)
    dma = pltpu.SemaphoreType.DMA
    return pl.pallas_call(
        functools.partial(fused_kernel, (n, SPAN, head, ffn, block, sub)),
        out_shape=jax.ShapeDtypeStruct((SPAN, block), bf16),
        in_specs=[anywhere, vmem] + [anywhere] * 8 + [vmem] * 3,
        out_specs=vmem,
        scratch_shapes=[
            pltpu.VMEM(inputs.shape, bf16),
            pltpu.VMEM((n, SPAN, block), bf16),
            pltpu.VMEM((block, width), bf16),
            pltpu.VMEM(w_out.shape, bf16),
            pltpu.VMEM(w_down.shape, bf16),
            pltpu.VMEM((cache, head), bf16),
            pltpu.VMEM((cache, head), bf16),
            pltpu.VMEM((n, SPAN, width), bf16),
            pltpu.VMEM((SPAN, width), f32),
            pltpu.VMEM((n, SPAN, width), bf16),
            pltpu.VMEM((n, SPAN, head), bf16),
            pltpu.VMEM((n, SPAN, ffn), bf16),
            pltpu.VMEM((n, SPAN, block), f32),
            pltpu.VMEM((n, SPAN, block), bf16),
            pltpu.VMEM((n, SPAN, block), bf16),
            pltpu.VMEM((n, SPAN, block), bf16),
            dma((GATHER_CHUNKS,)),
            dma((9,)),
            dma((n, 2)),
            dma((n, 2)),
            dma((n, 2)),
            dma((n, 2)),
            dma((n, GATHER_CHUNKS)),
            dma((n, GATHER_CHUNKS)),
            dma((n, GATHER_CHUNKS)),
            dma((n, GATHER_CHUNKS)),
            dma((n, GATHER_CHUNKS)),
            dma((n, 2)),
            dma((n, 2)),
            dma((n, REDUCE_CHUNKS)),
            dma((n, REDUCE_CHUNKS)),
            dma((n, REDUCE_CHUNKS)),
        ],
        compiler_params=pltpu.CompilerParams(
            collective_id=0, has_side_effects=True, vmem_limit_bytes=62 * 1024 * 1024
        ),
    )(
        inputs,
        ln_gain[None, :],
        w_query,
        w_keyval[0],
        w_gate,
        w_up,
        w_out,
        w_down,
        cache_keys[0],
        cache_values[0],
        cosine,
        sine,
        bias[None, :],
    )


def solution(mesh):
    fits = mesh.shape["tensor"] == mesh.shape["dp"] == 4 and mesh.shape["groups"] == 2
    return jax.shard_map(
        fused_on_device if fits else on_device,
        mesh=mesh,
        in_specs=(
            P(("groups", "tensor"), None),
            P(),
            P("dp", "tensor"),
            P("dp", "tensor", None),
            P("dp", "tensor"),
            P("dp", "tensor"),
            P("tensor", "dp"),
            P("tensor", "dp"),
            P(("groups", "dp"), None, None, None),
            P(("groups", "dp"), None, None, None),
            P(("groups", "dp")),
            P(("groups", "dp")),
        ),
        out_specs=P(("groups", "tensor"), "dp"),
        check_vma=False,
    )
```
